512 devices in a mesh: row: 32 (over z, x), col: 16 (over y, core).
Axes of the slice: x: 4, y: 8, z: 8, core: 2. Of those that a mesh axis runs over, the one named last changes fastest.
Arguments:
- states: float32 [512, 16, 256], P(('row', 'col')), may hold values from -170 to 170
- direction: float32 [512, 16, 256], P(('row', 'col')), may hold values from -170 to 170
- blocks: float32 [32, 16, 16, 256, 256], P('row', 'col'), may hold values from -0.09375 to 0.09375
- counts: int32 [32, 16], P('row', 'col'), may hold values from 4 to 16, as said below
- block_rows: int32 [32, 16, 16], P('row', 'col'), may hold values from 0 to 15, as said below
- block_cols: int32 [32, 16, 16], P('row', 'col'), may hold values from 0 to 31
- rotation: float32 [48, 16], replicated, may hold values from -0.875 to 0.875
Outputs:
- new_states: float32 [512, 16, 256], P(('row', 'col'))
- new_direction: float32 [512, 16, 256], P(('row', 'col'))
- quotient: float32 [16], replicated
The draws below stay inside these ranges and needn't reach their ends.
Inputs may be any that keep to these rules, and one draw needn't show every extreme that they name: `counts`: slots at or past an owner's count are unused; some owner fills all 16 slots. `block_rows`: several slots of an owner may name the same position.
All inputs are finite; a program needn't handle non-finite values.
Results may differ from the reference program's by a relative error of at most 0.0003.
Values sent between devices are 32-bit elements; how exact they have to be, the bound alone decides.
A program may use at most 64 MiB of HBM per device.

```python
import math
import jax
import jax.numpy as jnp
from jax import lax

BS = 256
K = 16
PB = 1
CAP = 16
GRID_R = 32
GRID_C = 16
ROW_BLOCKS = 16
COL_BLOCKS = 32
NBLK = 512
DIM = 131072
NSUB = 48


def scale_field(key, trend):
    first, second = jax.random.split(key)
    rough = jnp.exp(jax.random.uniform(first, (NBLK, 1, BS), jnp.float32) * math.log(10.0))
    position = (jnp.arange(NBLK * BS, dtype=jnp.float32) / (NBLK * BS)).reshape(NBLK, 1, BS)
    columns = jnp.exp(jax.random.uniform(second, (1, K, 1), jnp.float32) * math.log(3.0))
    return 0.2 * rough * columns * jnp.exp(position * math.log(trend))


def draw_states(key, part):
    key = jax.random.fold_in(key, 11)
    first, second = jax.random.split(key, 2)
    scales = scale_field(first, 3.0)
    noise = jax.random.truncated_normal(second, -4.0, 4.0, (NBLK, K, BS), jnp.float32)
    return scales * noise


def draw_direction(key, part):
    key = jax.random.fold_in(key, 17)
    first, second = jax.random.split(key, 2)
    scales = scale_field(first, 3.0)
    noise = jax.random.truncated_normal(second, -4.0, 4.0, (NBLK, K, BS), jnp.float32)
    return scales * noise


def draw_counts(key, part):
    key = jax.random.fold_in(key, 21)
    first, second = jax.random.split(key)
    loads = jax.random.randint(first, (GRID_R * GRID_C,), CAP // 4, CAP + 1)
    busiest = jax.random.randint(second, (), 0, GRID_R * GRID_C)
    owners = jnp.arange(GRID_R * GRID_C, dtype=jnp.int32)
    filled = jnp.where(owners == busiest, CAP, loads)
    return filled.reshape(GRID_R, GRID_C).astype(jnp.int32)


def spread_slots(key, limit):
    picks = jax.random.randint(key, (GRID_R * GRID_C, CAP), 0, limit)
    owners = jnp.arange(GRID_R * GRID_C, dtype=jnp.int32)
    first_slot = jnp.where(owners == 0, limit - 1, jnp.where(owners == 1, 0, picks[:, 0]))
    picks = picks.at[:, 0].set(first_slot)
    return picks.reshape(GRID_R, GRID_C, CAP).astype(jnp.int32)


def draw_block_rows(key, part):
    key = jax.random.fold_in(key, 31)
    return spread_slots(key, ROW_BLOCKS)


def draw_block_cols(key, part):
    key = jax.random.fold_in(key, 41)
    return spread_slots(key, COL_BLOCKS)


def steps_of(stream_key, shape, cuts, low, high):
    loudness, own = 1.0, jax.random.fold_in(stream_key, 6)
    for dim, shards_of in cuts:
        heights = jnp.exp(jax.random.uniform(jax.random.fold_in(own, dim), (shards_of,), jnp.float32, low / len(cuts), high / len(cuts)))
        loudness = loudness * jnp.repeat(heights, shape[dim] // shards_of).reshape([-1 if axis == dim else 1 for axis in range(len(shape))])
    return loudness


def normal_values(own_key, shape, spread, reach, shards=(), kind=jnp.bfloat16):
    result = jax.random.normal(own_key, shape, jnp.float32) * spread
    if len(shards) > 0:
        result = steps_of(own_key, shape, shards, -0.22, 0.18) * result
    return jnp.clip(result, min=-reach, max=reach).astype(kind)


def setup_inputs(seed: int = 0) -> dict:
    seeds = jax.random.split(jax.random.key(seed), 8)
    states = draw_states(jax.random.fold_in(seeds[7], 71), 0)
    direction = draw_direction(jax.random.fold_in(seeds[7], 71), 0)
    blocks = normal_values(seeds[2], (GRID_R, GRID_C, CAP, BS, BS), (BS * CAP) ** -0.5, 0.09375, ((0, 32), (1, 16)), jnp.float32)
    counts = draw_counts(jax.random.fold_in(seeds[7], 71), 0)
    block_rows = draw_block_rows(jax.random.fold_in(seeds[7], 71), 0)
    block_cols = draw_block_cols(jax.random.fold_in(seeds[7], 71), 0)
    rotation = normal_values(seeds[6], (NSUB, K), NSUB ** -0.5, 0.875, (), jnp.float32)
    return {"states": states, "direction": direction, "blocks": blocks, "counts": counts, "block_rows": block_rows, "block_cols": block_cols, "rotation": rotation}


PRECISE = lax.Precision.HIGHEST

def apply_hamiltonian(states, blocks, counts, block_rows, block_cols):
    total_slots = GRID_R * GRID_C * CAP
    flat_blocks = blocks.reshape(total_slots, BS, BS)
    slot_ids = jnp.arange(total_slots, dtype=jnp.int32)
    owner = slot_ids // CAP
    slot_in_owner = slot_ids % CAP
    owner_row = owner // GRID_C
    owner_col = owner % GRID_C
    alive = slot_in_owner < counts.reshape(-1)[owner]
    local_rows = block_rows.reshape(-1)
    local_cols = block_cols.reshape(-1)
    global_rows = (owner_row * ROW_BLOCKS + local_rows).astype(jnp.int32)
    global_cols = ((local_cols // PB * GRID_C + owner_col) * PB + local_cols % PB).astype(jnp.int32)

    def visit_slot(index, applied):
        matrix = flat_blocks[index]
        weight = jnp.where(alive[index], 1.0, 0.0).astype(states.dtype)
        target_row = global_rows[index]
        target_col = global_cols[index]
        forward = jnp.einsum('kj,ij->ki', states[target_col], matrix, precision=PRECISE)
        backward = jnp.dot(states[target_row], matrix, precision=PRECISE)
        applied = applied.at[target_row].add(weight * forward)
        applied = applied.at[target_col].add(weight * backward)
        return applied
    return lax.fori_loop(0, total_slots, visit_slot, jnp.zeros_like(states))

def reference(states, direction, blocks, counts, block_rows, block_cols, rotation):
    applied = apply_hamiltonian(states, blocks, counts, block_rows, block_cols)
    cross = jnp.sum(states * applied, axis=(0, 2))
    squares = jnp.sum(states * states, axis=(0, 2))
    quotient = cross / squares
    residual = applied - quotient[None, :, None] * states
    subspace = jnp.concatenate([states, residual, direction], axis=1)
    gram_matrix = jnp.einsum('bit,bjt->ij', subspace, subspace, precision=PRECISE) / DIM
    factor = jnp.linalg.cholesky(gram_matrix)
    flat_subspace = subspace.transpose(1, 0, 2).reshape(NSUB, DIM)
    basis = jax.scipy.linalg.solve_triangular(factor, flat_subspace, lower=True)
    tail_rows = jnp.concatenate([jnp.zeros((K, K), rotation.dtype), rotation[K:]], axis=0)
    new_flat = jnp.dot(rotation.T, basis, precision=PRECISE)
    tail_flat = jnp.dot(tail_rows.T, basis, precision=PRECISE)
    new_states = new_flat.reshape(K, NBLK, BS).transpose(1, 0, 2)
    new_direction = tail_flat.reshape(K, NBLK, BS).transpose(1, 0, 2)
    return (new_states, new_direction, quotient)
```

```python
import functools

import jax
import jax.numpy as jnp
from jax import lax
from jax.experimental import pallas as pl
from jax.experimental.pallas import tpu as pltpu
from jax.sharding import PartitionSpec as P

MESH = pl.DeviceIdType.MESH
HIGHEST = lax.Precision.HIGHEST
NX, NY, NZ, NC = 4, 8, 8, 2
SLOTS, K, BS, NSUB = 16, 16, 256, 48
F32, BF16 = jnp.float32, jnp.bfloat16

GZ, GX, GY, GC, RX, RZ, RC, RY = range(8)
EARLY, CROSS, LATE = 8, 12, 16
STAGES = 20


def dot(a, b, ca=1, cb=0, precision=HIGHEST):
    return lax.dot_general(a, b, (((ca,), (cb,)), ((), ())), precision=precision, preferred_element_type=F32)


def split(v):
    high = v.astype(BF16)
    return high, (v - high.astype(F32)).astype(BF16)


def inverse_factor(gram, order):
    rows = lax.broadcasted_iota(jnp.int32, (order, 1), 0)
    eye = (
        lax.broadcasted_iota(jnp.int32, (order, order), 0) == lax.broadcasted_iota(jnp.int32, (order, order), 1)
    ).astype(F32)
    work = jnp.concatenate([gram, eye], axis=1)
    for j in range(order - 1):
        pivot_row = work[j : j + 1, :]
        factor = jnp.where(rows > j, work[:, j : j + 1] / work[j : j + 1, j : j + 1], 0.0)
        work = work - factor * pivot_row
    pivots = jnp.sum(work[:, :order] * eye, axis=1, keepdims=True)
    return work[:, order:] / jnp.sqrt(pivots)


def kernel(
    states_hbm, direction_hbm, blocks_hbm, count_hbm, rows_hbm, cols_hbm, rotation_hbm,
    new_states_ref, new_direction_ref, quotient_ref,
    mat, high, low, xr, xc, products, pb, pf, rbx, rbz, rfc, rfy, direction, ar_c, ar_x, ar_y, ar_z,
    count_ref, rows_ref, cols_ref, rotation_ref, load_sem, block_sem, send_sem, recv_sem,
):
    row, col = lax.axis_index("row"), lax.axis_index("col")
    z, x = lax.div(row, NX), lax.rem(row, NX)
    y, core = lax.div(col, NC), lax.rem(col, NC)
    x_peers = [((lax.rem(x + d, NX)), (z * NX + lax.rem(x + d, NX), col)) for d in range(1, NX)]
    z_peers = [((lax.rem(z + d, NZ)), (lax.rem(z + d, NZ) * NX + x, col)) for d in range(1, NZ)]
    y_peers = [((lax.rem(y + d, NY)), (row, lax.rem(y + d, NY) * NC + core)) for d in range(1, NY)]
    c_peers = [(1 - core, (row, y * NC + 1 - core))]

    def load(src, dst, index):
        return pltpu.make_async_copy(src, dst, load_sem.at[index])

    def block_load(s):
        return pltpu.make_async_copy(blocks_hbm.at[0, 0, s], mat.at[s], block_sem.at[s])

    def send(stage, src, dst, device):
        pltpu.make_async_remote_copy(
            src_ref=src, dst_ref=dst, send_sem=send_sem.at[stage], recv_sem=recv_sem.at[stage],
            device_id=device, device_id_type=MESH,
        ).start()

    def arrived(stage, like):
        pltpu.make_async_copy(like, like, recv_sem.at[stage]).wait()

    def sent(stage, like):
        pltpu.make_async_copy(like, like, send_sem.at[stage]).wait()

    loads = [
        load(states_hbm.at[0], xr.at[x, z], 0),
        load(states_hbm.at[0], xc.at[core, y], 1),
        load(direction_hbm.at[0], direction, 2),
        load(count_hbm, count_ref, 3),
        load(rows_hbm, rows_ref, 4),
        load(cols_hbm, cols_ref, 5),
        load(rotation_hbm, rotation_ref, 6),
    ]
    for copy in loads:
        copy.start()
    for s in range(SLOTS):
        block_load(s).start()

    barrier = pltpu.get_barrier_semaphore()
    peers = [device for _, device in x_peers + z_peers + y_peers + c_peers]
    for device in peers:
        pl.semaphore_signal(barrier, inc=1, device_id=device, device_id_type=MESH)
    pl.semaphore_wait(barrier, len(peers))

    loads[0].wait()
    loads[1].wait()
    for _, device in z_peers:
        send(GZ, xr.at[x, z], xr.at[x, z], device)
    for _, device in y_peers:
        send(GY, xc.at[core, y], xc.at[core, y], device)

    ar_stages = [(ar_c, core, c_peers, NC), (ar_x, x, x_peers, NX), (ar_y, y, y_peers, NY), (ar_z, z, z_peers, NZ)]

    def ar_send(which, stage, value):
        buffer, me, others, _ = ar_stages[stage]
        place = (which - EARLY) // 4
        buffer[place, me] = value
        for _, device in others:
            send(which + stage, buffer.at[place, me], buffer.at[place, me], device)

    def ar_sum(which, stage):
        buffer, _, _, n = ar_stages[stage]
        place = (which - EARLY) // 4
        arrived(which + stage, buffer.at[place, 0 : n - 1])
        total = buffer[place, 0]
        for i in range(1, n):
            total = total + buffer[place, i]
        return total

    def ar_next(which, stage):
        ar_send(which, stage + 1, ar_sum(which, stage))

    states = xr[x, z]
    loads[2].wait()
    directions = direction[...]
    both = jnp.concatenate([states, directions], axis=0)
    gram = dot(both, both, 1, 1)
    ar_send(EARLY, 0, jnp.concatenate([gram[0:8], gram[8:16], gram[16:24], gram[24:32]], axis=1))

    def convert(s, carry):
        block_load(s).wait()
        h, l = split(mat[s])
        high[s] = h
        low[s] = l
        return carry

    lax.fori_loop(0, SLOTS // 2, convert, 0)
    arrived(GY, xc.at[core, 0 : NY - 1])
    send(GC, xc.at[core], xc.at[core], c_peers[0][1])
    ar_next(EARLY, 0)
    arrived(GZ, xr.at[x, 0 : NZ - 1])
    for _, device in x_peers:
        send(GX, xr.at[x], xr.at[x], device)
    lax.fori_loop(SLOTS // 2, SLOTS, convert, 0)
    ar_next(EARLY, 1)

    for copy in loads[3:6]:
        copy.wait()
    live = count_ref[0, 0]

    arrived(GC, xc.at[core])

    def backward(s, carry):
        place = rows_ref[0, 0, s]
        alive = jnp.where(s < live, 1.0, 0.0)
        source = xc[lax.rem(place, NC), lax.div(place, NC)] * alive
        h, l = split(source)
        both = dot(jnp.concatenate([h, l], axis=0), high[s], 1, 0, None)
        products[s] = both[:K] + both[K:] + dot(h, low[s], 1, 0, None)
        return carry

    lax.fori_loop(0, SLOTS, backward, 0)

    def pick(target, wanted, index_ref):
        total = jnp.zeros((K, BS), F32)
        for s in range(SLOTS):
            total = total + jnp.where(index_ref[0, 0, s] == wanted, 1.0, 0.0) * products[s]
        return total

    for index, device in x_peers + [(x, None)]:

        def fill(zz, carry, index=index):
            pb[index, zz] = pick(pb, zz * NX + index, cols_ref)
            return carry

        lax.fori_loop(0, NZ, fill, 0)
        if device is not None:
            send(RX, pb.at[index], rbx.at[x], device)

    ar_next(EARLY, 2)

    arrived(GX, xr.at[0 : NX - 1])

    def crossing(s, total):
        place = cols_ref[0, 0, s]
        return total + products[s] * xr[lax.rem(place, NX), lax.div(place, NX)]

    cross = lax.fori_loop(0, SLOTS, crossing, jnp.zeros((K, BS), F32))
    cross = 2.0 * jnp.sum(cross, axis=1, keepdims=True)
    lanes = lax.broadcasted_iota(jnp.int32, (8, 128), 1)
    ar_send(CROSS, 0, jnp.where(lanes < 64, cross[:8], cross[8:]))

    def forward(s, carry):
        place = cols_ref[0, 0, s]
        alive = jnp.where(s < live, 1.0, 0.0)
        source = xr[lax.rem(place, NX), lax.div(place, NX)] * alive
        h, l = split(source)
        both = dot(jnp.concatenate([h, l], axis=0), high[s], 1, 1, None)
        products[s] = both[:K] + both[K:] + dot(h, low[s], 1, 1, None)
        return carry

    lax.fori_loop(0, SLOTS, forward, 0)
    for index, device in c_peers + [(core, None)]:

        def fill(yy, carry, index=index):
            pf[index, yy] = pick(pf, yy * NC + index, rows_ref)
            return carry

        lax.fori_loop(0, NY, fill, 0)
        if device is not None:
            send(RC, pf.at[index], rfc, device)
    ar_next(CROSS, 0)

    arrived(RX, rbx.at[0 : NX - 1])

    def sum_x(zz, carry):
        total = pb[x, zz]
        for d in range(1, NX):
            total = total + rbx[lax.rem(x + d, NX), zz]
        pb[x, zz] = total
        return carry

    lax.fori_loop(0, NZ, sum_x, 0)
    for index, device in z_peers:
        send(RZ, pb.at[x, index], rbz.at[z], device)

    arrived(RC, rfc)

    def sum_c(yy, carry):
        pf[core, yy] = pf[core, yy] + rfc[yy]
        return carry

    lax.fori_loop(0, NY, sum_c, 0)
    for index, device in y_peers:
        send(RY, pf.at[core, index], rfy.at[y], device)
    ar_next(CROSS, 1)

    total_rows = BS * NZ * NX * NY * NC
    packed = ar_sum(EARLY, 3) / total_rows
    gram = jnp.concatenate([packed[:, 32 * i : 32 * i + 32] for i in range(4)], axis=0)
    squares = jnp.sum(
        jnp.where(
            lax.broadcasted_iota(jnp.int32, (K, K), 0) == lax.broadcasted_iota(jnp.int32, (K, K), 1),
            gram[:K, :K], 0.0,
        ),
        axis=1, keepdims=True,
    )
    inverse = inverse_factor(gram[:K, :K], K)
    basis = dot(inverse, states)
    project = dot(gram[K:, :K], inverse, 1, 1)
    rest = directions - dot(project, basis)
    gram_rest = gram[K:, K:] - dot(project, project, 1, 1)
    loads[6].wait()
    rotation = rotation_ref[...]
    kept = dot(rotation[:, :K], basis)

    ar_next(CROSS, 2)
    arrived(RY, rfy.at[0 : NY - 1])
    applied = pf[core, y]
    for d in range(1, NY):
        applied = applied + rfy[lax.rem(y + d, NY)]
    arrived(RZ, rbz.at[0 : NZ - 1])
    applied = applied + pb[x, z]
    for d in range(1, NZ):
        applied = applied + rbz[lax.rem(z + d, NZ)]
    crossed = ar_sum(CROSS, 3)
    quotient = jnp.concatenate([crossed[:, 0:1], crossed[:, 64:65]], axis=0) / (squares * total_rows)
    residual = applied - quotient * states
    quotient_ref[...] = jnp.sum(
        jnp.where(
            lax.broadcasted_iota(jnp.int32, (K, K), 0) == lax.broadcasted_iota(jnp.int32, (K, K), 1), quotient, 0.0
        ),
        axis=0, keepdims=True,
    )

    left = jnp.concatenate([residual, rest], axis=0)
    right = jnp.concatenate([basis, residual, rest], axis=0)
    local = dot(left, right, 1, 1)
    wide = jnp.concatenate([local[:K], local[K:, K : 2 * K]], axis=1)
    ar_send(LATE, 0, jnp.concatenate([wide[:8], wide[8:]], axis=1))
    ar_next(LATE, 0)
    ar_next(LATE, 1)
    ar_next(LATE, 2)
    packed = ar_sum(LATE, 3) / total_rows
    wide = jnp.concatenate([packed[:, :64], packed[:, 64:]], axis=0)
    lower = wide[:, :K]
    gram_residual = wide[:, K : 2 * K] - dot(lower, lower, 1, 1)
    top = jnp.concatenate([gram_residual, wide[:, 2 * K : 3 * K]], axis=1)
    bottom = jnp.concatenate([wide[:, 3 * K :], gram_rest], axis=1)
    inverse = inverse_factor(jnp.concatenate([top, bottom], axis=0), 2 * K)
    mixing = dot(rotation[:, K:], inverse)
    mixing = jnp.concatenate([-dot(mixing[:, :K], lower), mixing], axis=1)
    fresh = dot(mixing, right)
    new_direction_ref[0] = fresh
    new_states_ref[0] = kept + new_direction_ref[0]

    sent(GZ, xr.at[x, 0 : NZ - 1])
    sent(GX, xr.at[0 : NX - 1])
    sent(GY, xc.at[core, 0 : NY - 1])
    sent(GC, xc.at[core])
    sent(RX, rbx.at[0 : NX - 1])
    sent(RZ, rbz.at[0 : NZ - 1])
    sent(RC, rfc)
    sent(RY, rfy.at[0 : NY - 1])
    for which in (EARLY, CROSS, LATE):
        for stage in range(4):
            buffer, _, _, n = ar_stages[stage]
            sent(which + stage, buffer.at[0, 0 : n - 1])


def body(states, direction, blocks, counts, block_rows, block_cols, rotation):
    vmem = pl.BlockSpec(memory_space=pltpu.VMEM)
    hbm = pl.BlockSpec(memory_space=pl.ANY)
    new_states, new_direction, quotient = pl.pallas_call(
        kernel,
        out_shape=(
            jax.ShapeDtypeStruct((1, K, BS), F32),
            jax.ShapeDtypeStruct((1, K, BS), F32),
            jax.ShapeDtypeStruct((1, K), F32),
        ),
        in_specs=[hbm] * 7,
        out_specs=(vmem, vmem, vmem),
        scratch_shapes=[
            pltpu.VMEM((SLOTS, BS, BS), F32),
            pltpu.VMEM((SLOTS, BS, BS), BF16),
            pltpu.VMEM((SLOTS, BS, BS), BF16),
            pltpu.VMEM((NX, NZ, K, BS), F32),
            pltpu.VMEM((NC, NY, K, BS), F32),
            pltpu.VMEM((SLOTS, K, BS), F32),
            pltpu.VMEM((NX, NZ, K, BS), F32),
            pltpu.VMEM((NC, NY, K, BS), F32),
            pltpu.VMEM((NX, NZ, K, BS), F32),
            pltpu.VMEM((NZ, K, BS), F32),
            pltpu.VMEM((NY, K, BS), F32),
            pltpu.VMEM((NY, K, BS), F32),
            pltpu.VMEM((K, BS), F32),
            pltpu.VMEM((3, NC, 8, 128), F32),
            pltpu.VMEM((3, NX, 8, 128), F32),
            pltpu.VMEM((3, NY, 8, 128), F32),
            pltpu.VMEM((3, NZ, 8, 128), F32),
            pltpu.SMEM((1, 1), jnp.int32),
            pltpu.SMEM((1, 1, SLOTS), jnp.int32),
            pltpu.SMEM((1, 1, SLOTS), jnp.int32),
            pltpu.VMEM((K, NSUB), F32),
            pltpu.SemaphoreType.DMA((7,)),
            pltpu.SemaphoreType.DMA((SLOTS,)),
            pltpu.SemaphoreType.DMA((STAGES,)),
            pltpu.SemaphoreType.DMA((STAGES,)),
        ],
        compiler_params=pltpu.CompilerParams(
            collective_id=0, has_side_effects=True, vmem_limit_bytes=60 * 1024 * 1024
        ),
    )(states, direction, blocks, counts, block_rows, block_cols, rotation.T)
    return new_states, new_direction, quotient.reshape(K)


def solution(mesh):
    return jax.shard_map(
        body,
        mesh=mesh,
        in_specs=(
            P(("row", "col"), None, None),
            P(("row", "col"), None, None),
            P("row", "col", None, None, None),
            P("row", "col"),
            P("row", "col", None),
            P("row", "col", None),
            P(),
        ),
        out_specs=(P(("row", "col"), None, None), P(("row", "col"), None, None), P()),
        check_vma=False,
    )
```

```python
import jax
import jax.numpy as jnp
from jax import lax
from jax.experimental import pallas as pl
from jax.experimental.pallas import tpu as pltpu
from jax.sharding import PartitionSpec as P

MESH = pl.DeviceIdType.MESH
HIGHEST = lax.Precision.HIGHEST
NX, NY, NZ, NC = 4, 8, 8, 2
SLOTS, K, BS, NSUB = 16, 16, 256, 48
F32, BF16 = jnp.float32, jnp.bfloat16
GATHER_GROUPS = ((0, 1), (1, 3), (3, 5), (5, 8))
SCATTER_GROUPS = ((3, 8), (0, 3))
X_ORDER = (2, 1, 3)
STAGES = 64


def place_of(offset):
    return jnp.where(offset <= NZ // 2, jnp.maximum(2 * offset - 1, 0), 2 * (NZ - offset))


def offset_of(place):
    return jnp.where(lax.rem(place, 2) == 1, lax.div(place + 1, 2), lax.rem(NZ - lax.div(place, 2), NZ))


PLACE = [0 if d == 0 else 2 * d - 1 if d <= NZ // 2 else 2 * (NZ - d) for d in range(NZ)]


def dot(a, b, ca=1, cb=0, precision=HIGHEST):
    return lax.dot_general(a, b, (((ca,), (cb,)), ((), ())), precision=precision, preferred_element_type=F32)


def split(v):
    high = v.astype(BF16)
    return high, (v - high.astype(F32)).astype(BF16)


def identity(order):
    return (
        lax.broadcasted_iota(jnp.int32, (order, order), 0) == lax.broadcasted_iota(jnp.int32, (order, order), 1)
    ).astype(F32)


def inverse_factor(gram, order):
    shape = (order, 128)
    rows = lax.broadcasted_iota(jnp.int32, shape, 0)
    eye = identity(order)
    work = jnp.concatenate([gram, eye, jnp.zeros((order, 128 - 2 * order), F32)], axis=1)

    def wide(part):
        return jnp.broadcast_to(part, shape)

    for j in range(0, order, 2):
        u, v = wide(work[:, j : j + 1]), wide(work[:, j + 1 : j + 2])
        first, second = wide(work[j : j + 1, :]), wide(work[j + 1 : j + 2, :])
        a, b, c = wide(u[j : j + 1, :]), wide(v[j : j + 1, :]), wide(v[j + 1 : j + 2, :])
        scale = 1.0 / (a * c - b * b)
        below = u * ((c * first - b * second) * scale) + v * ((a * second - b * first) * scale)
        work = work - jnp.where(rows > j + 1, below, jnp.where(rows == j + 1, (b / a) * first, 0.0))
    pivots = jnp.sum(work[:, :order] * eye, axis=1, keepdims=True)
    return work[:, order : 2 * order] / jnp.sqrt(pivots)


def kernel(
    states_hbm, direction_hbm, blocks_hbm, count_hbm, rows_hbm, cols_hbm, rotation_hbm,
    new_states_ref, new_direction_ref, quotient_ref,
    mat, high, low, xr, xc, products, pb, pf, rbx, rbz, rfc, rfy, direction,
    ar_c, ar_x, ar_y, ar_z, count_ref, rows_ref, cols_ref, rotation_ref, load_sem, block_sem, send_sem, recv_sem,
):
    row, col = lax.axis_index("row"), lax.axis_index("col")
    z, x = lax.div(row, NX), lax.rem(row, NX)
    y, core = lax.div(col, NC), lax.rem(col, NC)
    x_peers = [(z * NX + lax.rem(x + d, NX), col) for d in range(1, NX)]
    z_order = sorted(range(1, NZ), key=lambda d: -min(d, NZ - d))
    z_peers = [(lax.rem(z + d, NZ) * NX + x, col) for d in z_order]
    y_peers = [(lax.rem(y + d, NY), (row, lax.rem(y + d, NY) * NC + core)) for d in sorted(range(1, NY), key=lambda d: -min(d, NY - d))]
    other_core = (row, y * NC + 1 - core)

    stages, drains = {}, []

    def stage_of(name):
        return stages.setdefault(name, len(stages))

    def load(src, dst, index):
        return pltpu.make_async_copy(src, dst, load_sem.at[index])

    def block_load(s):
        return pltpu.make_async_copy(blocks_hbm.at[0, 0, s], mat.at[s], block_sem.at[s])

    def send(name, src, dst, device, recv_name=None):
        pltpu.make_async_remote_copy(
            src_ref=src, dst_ref=dst, send_sem=send_sem.at[stage_of(name)],
            recv_sem=recv_sem.at[stage_of(recv_name or name)], device_id=device, device_id_type=MESH,
        ).start()

    def send_one(name, src, dst, device):
        send(name, src, dst, device)
        drains.append((name, src))

    def arrived(name, like):
        pltpu.make_async_copy(like, like, recv_sem.at[stage_of(name)]).wait()

    loads = [
        load(states_hbm.at[0], xr.at[x, 0], 0),
        load(states_hbm.at[0], xc.at[core, y], 1),
        load(direction_hbm.at[0], direction, 2),
        load(count_hbm, count_ref, 3),
        load(rows_hbm, rows_ref, 4),
        load(cols_hbm, cols_ref, 5),
        load(rotation_hbm, rotation_ref, 6),
    ]
    barrier = pltpu.get_barrier_semaphore()
    peers = z_peers + [device for _, device in y_peers] + x_peers + [other_core]
    for device in peers:
        pl.semaphore_signal(barrier, inc=1, device_id=device, device_id_type=MESH)
    for copy in loads:
        copy.start()
    for s in range(SLOTS):
        block_load(s).start()

    pl.semaphore_wait(barrier, len(peers))

    def gather_group(place):
        return [i for i, (a, b) in enumerate(GATHER_GROUPS) if a <= place < b][0]

    loads[0].wait()
    for d, device in zip(z_order, z_peers):
        there = PLACE[NZ - d]
        send("gz", xr.at[x, 0], xr.at[x, there], device, ("gz", gather_group(there)))
    drains.append(("gz", xr.at[0, 0 : NZ - 1]))
    def gather_x(g):
        a, b = GATHER_GROUPS[g]
        if g > 0:
            arrived(("gz", g), xr.at[x, a:b])
        for d in X_ORDER:
            send_one(("gx", d, g), xr.at[x, a:b], xr.at[x, a:b], x_peers[d - 1])

    ar_stages = [
        (ar_c, core, [other_core], NC), (ar_y, y, [device for _, device in y_peers], NY),
        (ar_z, z, z_peers, NZ), (ar_x, x, x_peers, NX),
    ]
    EARLY, CROSS, LATE = range(3)

    def ar_send(which, stage, value):
        buffer, me, others, n = ar_stages[stage]
        buffer[which, me] = value
        for device in others:
            send(("ar", which, stage), buffer.at[which, me], buffer.at[which, me], device)
        drains.append((("ar", which, stage), buffer.at[which, 0 : n - 1]))

    def ar_sum(which, stage):
        buffer, _, _, n = ar_stages[stage]
        arrived(("ar", which, stage), buffer.at[which, 0 : n - 1])
        total = [buffer[which, i] for i in range(n)]
        while len(total) > 1:
            total = [total[i] + total[i + 1] for i in range(0, len(total), 2)]
        return total[0]

    def ar_next(which, stage):
        ar_send(which, stage + 1, ar_sum(which, stage))

    def convert(s, carry):
        block_load(s).wait()
        h, l = split(mat[s])
        high[s] = h
        low[s] = l
        return carry

    gather_x(0)
    loads[1].wait()
    for _, device in y_peers:
        send("gy", xc.at[core, y], xc.at[core, y], device)
    drains.append(("gy", xc.at[0, 0 : NY - 1]))
    states = xr[x, 0]
    loads[2].wait()
    directions = direction[...]
    both = jnp.concatenate([states, directions], axis=0)
    gram = dot(both, both, 1, 1)
    ar_send(EARLY, 0, jnp.concatenate([gram[0:8], gram[8:16], gram[16:24], gram[24:32]], axis=1))
    for g in range(1, len(GATHER_GROUPS) - 1):
        gather_x(g)
    lax.fori_loop(0, SLOTS, convert, 0)
    gather_x(len(GATHER_GROUPS) - 1)
    arrived("gy", xc.at[0, 0 : NY - 1])
    send_one("gc", xc.at[core], xc.at[core], other_core)
    ar_next(EARLY, 0)
    for copy in loads[3:6]:
        copy.wait()
    live = count_ref[0, 0]

    arrived("gc", xc.at[core])

    def backward(s, carry):
        place = rows_ref[0, 0, s]
        alive = jnp.where(s < live, 1.0, 0.0)
        source = xc[lax.rem(place, NC), lax.div(place, NC)] * alive
        h, l = split(source)
        both = dot(jnp.concatenate([h, l], axis=0), high[s], 1, 0, None)
        products[s] = both[:K] + both[K:] + dot(h, low[s], 1, 0, None)
        return carry

    lax.fori_loop(0, SLOTS, backward, 0, unroll=4)

    def pick(wanted, index_ref):
        total = jnp.zeros((K, BS), F32)
        for s in range(SLOTS):
            total = total + jnp.where(index_ref[0, 0, s] == wanted, 1.0, 0.0) * products[s]
        return total

    def fill_plane(plane):
        def fill(place, carry):
            pb[plane, place] = pick(lax.rem(z + offset_of(place), NZ) * NX + plane, cols_ref)
            return carry

        lax.fori_loop(0, NZ, fill, 0)

    for d in X_ORDER:
        plane = lax.rem(x + d, NX)
        fill_plane(plane)
        for h, (a, b) in enumerate(SCATTER_GROUPS):
            send_one(("sx", d, h), pb.at[plane, a:b], rbx.at[d - 1, a:b], x_peers[d - 1])

    def scatter_z(h):
        a, b = SCATTER_GROUPS[h]
        for d in X_ORDER:
            arrived(("sx", d, h), rbx.at[d - 1, a:b])
        for p in range(a, b):
            total = pb[x, p]
            for d in range(1, NX):
                total = total + rbx[d - 1, p]
            pb[x, p] = total
        for d, device in zip(z_order, z_peers):
            if a <= PLACE[d] < b:
                send("sz", pb.at[x, PLACE[d]], rbz.at[PLACE[NZ - d]], device)

    ar_next(EARLY, 1)
    fill_plane(x)

    for g, (a, b) in enumerate(GATHER_GROUPS):
        for d in X_ORDER:
            arrived(("gx", d, g), xr.at[lax.rem(x + NX - d, NX), a:b])

    def column_rows(s):
        block = cols_ref[0, 0, s]
        return xr[lax.rem(block, NX), place_of(lax.rem(lax.div(block, NX) - z + NZ, NZ))]

    def crossing(s, total):
        return total + products[s] * column_rows(s)

    cross = lax.fori_loop(0, SLOTS, crossing, jnp.zeros((K, BS), F32), unroll=4)
    cross = 2.0 * jnp.sum(cross, axis=1, keepdims=True)
    lanes = lax.broadcasted_iota(jnp.int32, (8, 128), 1)
    ar_send(CROSS, 0, jnp.where(lanes < 64, cross[:8], cross[8:]))

    def forward(s, carry):
        alive = jnp.where(s < live, 1.0, 0.0)
        h, l = split(column_rows(s) * alive)
        both = dot(jnp.concatenate([h, l], axis=0), high[s], 1, 1, None)
        products[s] = both[:K] + both[K:] + dot(h, low[s], 1, 1, None)
        return carry

    lax.fori_loop(0, SLOTS // 2, forward, 0, unroll=4)
    ar_next(CROSS, 0)
    lax.fori_loop(SLOTS // 2, SLOTS, forward, 0, unroll=4)

    def fill_core(half):
        def fill(yy, carry):
            pf[half, yy] = pick(yy * NC + half, rows_ref)
            return carry

        lax.fori_loop(0, NY, fill, 0)

    fill_core(1 - core)
    send_one("sc", pf.at[1 - core], rfc, other_core)
    ar_next(EARLY, 2)
    fill_core(core)
    ar_next(CROSS, 1)
    scatter_z(0)
    arrived("sc", rfc)

    def sum_c(yy, carry):
        pf[core, yy] = pf[core, yy] + rfc[yy]
        return carry

    lax.fori_loop(0, NY, sum_c, 0)
    for index, device in y_peers:
        send("sy", pf.at[core, index], rfy.at[y], device)
    drains.append(("sy", pf.at[0, 0 : NY - 1]))
    scatter_z(1)
    drains.append(("sz", rbz.at[0 : NZ - 1]))

    total_rows = BS * NZ * NX * NY * NC
    packed = ar_sum(EARLY, 3) / total_rows
    gram = jnp.concatenate([packed[:, 32 * i : 32 * i + 32] for i in range(4)], axis=0)
    squares = jnp.sum(gram[:K, :K] * identity(K), axis=1, keepdims=True)
    inverse = inverse_factor(gram[:K, :K], K)
    basis = dot(inverse, states)
    project = dot(gram[K:, :K], inverse, 1, 1)
    rest = directions - dot(project, basis)
    gram_rest = gram[K:, K:] - dot(project, project, 1, 1)
    loads[6].wait()
    rotation = rotation_ref[...]
    kept = dot(rotation[:, :K], basis)

    ar_next(CROSS, 2)
    arrived("sy", rfy.at[0 : NY - 1])
    applied = pf[core, y]
    for d in range(1, NY):
        applied = applied + rfy[lax.rem(y + d, NY)]
    arrived("sz", rbz.at[0 : NZ - 1])
    applied = applied + pb[x, 0]
    for place in range(1, NZ):
        applied = applied + rbz[place]
    crossed = ar_sum(CROSS, 3)
    quotient = jnp.concatenate([crossed[:, 0:1], crossed[:, 64:65]], axis=0) / (squares * total_rows)
    residual = applied - quotient * states

    left_side = jnp.concatenate([residual, rest], axis=0)
    right_side = jnp.concatenate([basis, residual, rest], axis=0)
    local = dot(left_side, right_side, 1, 1)
    wide = jnp.concatenate([local[:K], local[K:, K : 2 * K]], axis=1)
    ar_send(LATE, 0, jnp.concatenate([wide[:8], wide[8:]], axis=1))
    quotient_ref[...] = jnp.sum(identity(K) * quotient, axis=0, keepdims=True)
    ar_next(LATE, 0)
    ar_next(LATE, 1)
    ar_next(LATE, 2)
    packed = ar_sum(LATE, 3) / total_rows
    wide = jnp.concatenate([packed[:, :64], packed[:, 64:]], axis=0)
    lower = wide[:, :K]
    gram_residual = wide[:, K : 2 * K] - dot(lower, lower, 1, 1)
    top = jnp.concatenate([gram_residual, wide[:, 2 * K : 3 * K]], axis=1)
    bottom = jnp.concatenate([wide[:, 3 * K :], gram_rest], axis=1)
    inverse = inverse_factor(jnp.concatenate([top, bottom], axis=0), 2 * K)
    mixing = dot(rotation[:, K:], inverse)
    mixing = jnp.concatenate([-dot(mixing[:, :K], lower), mixing], axis=1)
    fresh = dot(mixing, right_side)
    new_direction_ref[0] = fresh
    new_states_ref[0] = kept + new_direction_ref[0]

    for name, like in drains:
        pltpu.make_async_copy(like, like, send_sem.at[stage_of(name)]).wait()


def finish(states_hbm, direction_hbm, quotient_hbm, new_states_ref, new_direction_ref, quotient_ref, sem):
    copies = [
        pltpu.make_async_copy(states_hbm, new_states_ref, sem.at[0]),
        pltpu.make_async_copy(direction_hbm, new_direction_ref, sem.at[1]),
        pltpu.make_async_copy(quotient_hbm, quotient_ref, sem.at[2]),
    ]
    for copy in copies:
        copy.start()
    for copy in copies:
        copy.wait()


def body(states, direction, blocks, counts, block_rows, block_cols, rotation):
    vmem = pl.BlockSpec(memory_space=pltpu.VMEM)
    hbm = pl.BlockSpec(memory_space=pltpu.HBM)
    outs = (
        jax.ShapeDtypeStruct((1, K, BS), F32),
        jax.ShapeDtypeStruct((1, K, BS), F32),
        jax.ShapeDtypeStruct((1, K), F32),
    )
    results = pl.pallas_call(
        kernel,
        out_shape=outs,
        in_specs=[hbm] * 7,
        out_specs=(vmem, vmem, vmem),
        scratch_shapes=[
            pltpu.VMEM((SLOTS, BS, BS), F32),
            pltpu.VMEM((SLOTS, BS, BS), BF16),
            pltpu.VMEM((SLOTS, BS, BS), BF16),
            pltpu.VMEM((NX, NZ, K, BS), F32),
            pltpu.VMEM((NC, NY, K, BS), F32),
            pltpu.VMEM((SLOTS, K, BS), F32),
            pltpu.VMEM((NX, NZ, K, BS), F32),
            pltpu.VMEM((NC, NY, K, BS), F32),
            pltpu.VMEM((NX - 1, NZ, K, BS), F32),
            pltpu.VMEM((NZ, K, BS), F32),
            pltpu.VMEM((NY, K, BS), F32),
            pltpu.VMEM((NY, K, BS), F32),
            pltpu.VMEM((K, BS), F32),
            pltpu.VMEM((3, NC, 8, 128), F32),
            pltpu.VMEM((3, NX, 8, 128), F32),
            pltpu.VMEM((3, NY, 8, 128), F32),
            pltpu.VMEM((3, NZ, 8, 128), F32),
            pltpu.SMEM((1, 1), jnp.int32),
            pltpu.SMEM((1, 1, SLOTS), jnp.int32),
            pltpu.SMEM((1, 1, SLOTS), jnp.int32),
            pltpu.VMEM((K, NSUB), F32),
            pltpu.SemaphoreType.DMA((7,)),
            pltpu.SemaphoreType.DMA((SLOTS,)),
            pltpu.SemaphoreType.DMA((STAGES,)),
            pltpu.SemaphoreType.DMA((STAGES,)),
        ],
        compiler_params=pltpu.CompilerParams(
            collective_id=0, has_side_effects=True, vmem_limit_bytes=60 * 1024 * 1024
        ),
    )(states, direction, blocks, counts, block_rows, block_cols, rotation.T)
    new_states, new_direction, quotient = pl.pallas_call(
        finish,
        out_shape=outs,
        in_specs=[hbm] * 3,
        out_specs=(hbm,) * 3,
        scratch_shapes=[pltpu.SemaphoreType.DMA((3,))],
        compiler_params=pltpu.CompilerParams(vmem_limit_bytes=60 * 1024 * 1024),
    )(*results)
    return new_states, new_direction, quotient.reshape(K)


def solution(mesh):
    return jax.shard_map(
        body,
        mesh=mesh,
        in_specs=(
            P(("row", "col"), None, None),
            P(("row", "col"), None, None),
            P("row", "col", None, None, None),
            P("row", "col"),
            P("row", "col", None),
            P("row", "col", None),
            P(),
        ),
        out_specs=(P(("row", "col"), None, None), P(("row", "col"), None, None), P()),
        check_vma=False,
    )
```

```python
import jax
import jax.numpy as jnp
from jax import lax
from jax.experimental import pallas as pl
from jax.experimental.pallas import tpu as pltpu
from jax.sharding import PartitionSpec as P

MESH = pl.DeviceIdType.MESH
HIGHEST = lax.Precision.HIGHEST
NX, NY, NZ, NC = 4, 8, 8, 2
SLOTS, K, BS, NSUB = 16, 16, 256, 48
F32, BF16 = jnp.float32, jnp.bfloat16
GATHER_GROUPS = ((0, 1), (1, 3), (3, 5), (5, 8))
SCATTER_GROUPS = ((3, 8), (0, 3))
X_ORDER = (2, 1, 3)
STAGES = 64


def place_of(offset):
    return jnp.where(offset <= NZ // 2, jnp.maximum(2 * offset - 1, 0), 2 * (NZ - offset))


def offset_of(place):
    return jnp.where(lax.rem(place, 2) == 1, lax.div(place + 1, 2), lax.rem(NZ - lax.div(place, 2), NZ))


PLACE = [0 if d == 0 else 2 * d - 1 if d <= NZ // 2 else 2 * (NZ - d) for d in range(NZ)]


def dot(a, b, ca=1, cb=0, precision=HIGHEST):
    return lax.dot_general(a, b, (((ca,), (cb,)), ((), ())), precision=precision, preferred_element_type=F32)


def split(v):
    high = v.astype(BF16)
    return high, (v - high.astype(F32)).astype(BF16)


def identity(order):
    return (
        lax.broadcasted_iota(jnp.int32, (order, order), 0) == lax.broadcasted_iota(jnp.int32, (order, order), 1)
    ).astype(F32)


def inverse_factor(gram, order):
    shape = (order, 128)
    rows = lax.broadcasted_iota(jnp.int32, shape, 0)
    eye = identity(order)
    work = jnp.concatenate([gram, eye, jnp.zeros((order, 128 - 2 * order), F32)], axis=1)

    def wide(part):
        return jnp.broadcast_to(part, shape)

    for j in range(0, order, 2):
        u, v = wide(work[:, j : j + 1]), wide(work[:, j + 1 : j + 2])
        first, second = wide(work[j : j + 1, :]), wide(work[j + 1 : j + 2, :])
        a, b, c = wide(u[j : j + 1, :]), wide(v[j : j + 1, :]), wide(v[j + 1 : j + 2, :])
        scale = 1.0 / (a * c - b * b)
        below = u * ((c * first - b * second) * scale) + v * ((a * second - b * first) * scale)
        work = work - jnp.where(rows > j + 1, below, jnp.where(rows == j + 1, (b / a) * first, 0.0))
    pivots = jnp.sum(work[:, :order] * eye, axis=1, keepdims=True)
    return work[:, order : 2 * order] / jnp.sqrt(pivots)


def kernel(
    states_hbm, direction_hbm, blocks_hbm, count_hbm, rows_hbm, cols_hbm, rotation_hbm,
    new_states_ref, new_direction_ref, quotient_ref,
    mat, high, low, xr, xc, products, pb, pf, rbx, rbz, rfc, rfy, direction,
    ar_c, ar_x, ar_y, ar_z, count_ref, rows_ref, cols_ref, rotation_ref, load_sem, block_sem, send_sem, recv_sem,
):
    row, col = lax.axis_index("row"), lax.axis_index("col")
    z, x = lax.div(row, NX), lax.rem(row, NX)
    y, core = lax.div(col, NC), lax.rem(col, NC)
    x_peers = [(z * NX + lax.rem(x + d, NX), col) for d in range(1, NX)]
    z_order = sorted(range(1, NZ), key=lambda d: -min(d, NZ - d))
    z_peers = [(lax.rem(z + d, NZ) * NX + x, col) for d in z_order]
    y_peers = [(lax.rem(y + d, NY), (row, lax.rem(y + d, NY) * NC + core)) for d in sorted(range(1, NY), key=lambda d: -min(d, NY - d))]
    other_core = (row, y * NC + 1 - core)

    stages, drains = {}, []

    def stage_of(name):
        return stages.setdefault(name, len(stages))

    def load(src, dst, index):
        return pltpu.make_async_copy(src, dst, load_sem.at[index])

    def block_load(s):
        return pltpu.make_async_copy(blocks_hbm.at[0, 0, s], mat.at[s], block_sem.at[s])

    def send(name, src, dst, device, recv_name=None):
        pltpu.make_async_remote_copy(
            src_ref=src, dst_ref=dst, send_sem=send_sem.at[stage_of(name)],
            recv_sem=recv_sem.at[stage_of(recv_name or name)], device_id=device, device_id_type=MESH,
        ).start()

    def send_one(name, src, dst, device):
        send(name, src, dst, device)
        drains.append((name, src))

    def arrived(name, like):
        pltpu.make_async_copy(like, like, recv_sem.at[stage_of(name)]).wait()

    loads = [
        load(states_hbm.at[0], xr.at[x, 0], 0),
        load(states_hbm.at[0], xc.at[core, y], 1),
        load(direction_hbm.at[0], direction, 2),
        load(count_hbm, count_ref, 3),
        load(rows_hbm, rows_ref, 4),
        load(cols_hbm, cols_ref, 5),
        load(rotation_hbm, rotation_ref, 6),
    ]
    barrier = pltpu.get_barrier_semaphore()
    peers = z_peers + [device for _, device in y_peers] + x_peers + [other_core]
    for device in peers:
        pl.semaphore_signal(barrier, inc=1, device_id=device, device_id_type=MESH)
    for copy in loads:
        copy.start()
    for s in range(SLOTS):
        block_load(s).start()

    pl.semaphore_wait(barrier, len(peers))

    def gather_group(place):
        return [i for i, (a, b) in enumerate(GATHER_GROUPS) if a <= place < b][0]

    loads[0].wait()
    for d, device in zip(z_order, z_peers):
        there = PLACE[NZ - d]
        send("gz", xr.at[x, 0], xr.at[x, there], device, ("gz", gather_group(there)))
    drains.append(("gz", xr.at[0, 0 : NZ - 1]))
    def gather_x(g):
        a, b = GATHER_GROUPS[g]
        if g > 0:
            arrived(("gz", g), xr.at[x, a:b])
        for d in X_ORDER:
            send_one(("gx", d, g), xr.at[x, a:b], xr.at[x, a:b], x_peers[d - 1])

    ar_stages = [
        (ar_c, core, [other_core], NC), (ar_y, y, [device for _, device in y_peers], NY),
        (ar_z, z, z_peers, NZ), (ar_x, x, x_peers, NX),
    ]
    EARLY, CROSS, LATE = range(3)

    def ar_send(which, stage, value):
        buffer, me, others, n = ar_stages[stage]
        buffer[which, me] = value
        for device in others:
            send(("ar", which, stage), buffer.at[which, me], buffer.at[which, me], device)
        drains.append((("ar", which, stage), buffer.at[which, 0 : n - 1]))

    def ar_sum(which, stage):
        buffer, _, _, n = ar_stages[stage]
        arrived(("ar", which, stage), buffer.at[which, 0 : n - 1])
        total = [buffer[which, i] for i in range(n)]
        while len(total) > 1:
            total = [total[i] + total[i + 1] for i in range(0, len(total), 2)]
        return total[0]

    def ar_next(which, stage):
        ar_send(which, stage + 1, ar_sum(which, stage))

    def convert(s, carry):
        block_load(s).wait()
        h, l = split(mat[s])
        high[s] = h
        low[s] = l
        return carry

    gather_x(0)
    loads[1].wait()
    for _, device in y_peers:
        send("gy", xc.at[core, y], xc.at[core, y], device)
    drains.append(("gy", xc.at[0, 0 : NY - 1]))
    states = xr[x, 0]
    loads[2].wait()
    directions = direction[...]
    both = jnp.concatenate([states, directions], axis=0)
    gram = dot(both, both, 1, 1)
    ar_send(EARLY, 0, jnp.concatenate([gram[0:8], gram[8:16], gram[16:24], gram[24:32]], axis=1))
    for g in range(1, len(GATHER_GROUPS) - 1):
        gather_x(g)
    lax.fori_loop(0, SLOTS, convert, 0)
    gather_x(len(GATHER_GROUPS) - 1)
    arrived("gy", xc.at[0, 0 : NY - 1])
    send_one("gc", xc.at[core], xc.at[core], other_core)
    ar_next(EARLY, 0)
    for copy in loads[3:6]:
        copy.wait()
    live = count_ref[0, 0]

    arrived("gc", xc.at[core])

    def backward(s, carry):
        place = rows_ref[0, 0, s]
        alive = jnp.where(s < live, 1.0, 0.0)
        source = xc[lax.rem(place, NC), lax.div(place, NC)] * alive
        h, l = split(source)
        both = dot(jnp.concatenate([h, l], axis=0), high[s], 1, 0, None)
        products[s] = both[:K] + both[K:] + dot(h, low[s], 1, 0, None)
        return carry

    lax.fori_loop(0, SLOTS, backward, 0, unroll=4)

    def pick(wanted, index_ref):
        total = jnp.zeros((K, BS), F32)
        for s in range(SLOTS):
            total = total + jnp.where(index_ref[0, 0, s] == wanted, 1.0, 0.0) * products[s]
        return total

    def fill_plane(plane, first, end):
        def fill(place, carry):
            pb[plane, place] = pick(lax.rem(z + offset_of(place), NZ) * NX + plane, cols_ref)
            return carry

        lax.fori_loop(first, end, fill, 0)

    for h, (a, b) in enumerate(SCATTER_GROUPS):
        for d in X_ORDER:
            plane = lax.rem(x + d, NX)
            fill_plane(plane, a, b)
            send_one(("sx", d, h), pb.at[plane, a:b], rbx.at[d - 1, a:b], x_peers[d - 1])

    def scatter_z(h):
        a, b = SCATTER_GROUPS[h]
        for d in X_ORDER:
            arrived(("sx", d, h), rbx.at[d - 1, a:b])
        for p in range(a, b):
            total = pb[x, p]
            for d in range(1, NX):
                total = total + rbx[d - 1, p]
            pb[x, p] = total
        for d, device in zip(z_order, z_peers):
            if a <= PLACE[d] < b:
                send("sz", pb.at[x, PLACE[d]], rbz.at[PLACE[NZ - d]], device)

    ar_next(EARLY, 1)
    fill_plane(x, 0, NZ)

    for g, (a, b) in enumerate(GATHER_GROUPS):
        for d in X_ORDER:
            arrived(("gx", d, g), xr.at[lax.rem(x + NX - d, NX), a:b])

    def column_rows(s):
        block = cols_ref[0, 0, s]
        return xr[lax.rem(block, NX), place_of(lax.rem(lax.div(block, NX) - z + NZ, NZ))]

    def crossing(s, total):
        return total + products[s] * column_rows(s)

    cross = lax.fori_loop(0, SLOTS, crossing, jnp.zeros((K, BS), F32), unroll=4)
    cross = 2.0 * jnp.sum(cross, axis=1, keepdims=True)
    lanes = lax.broadcasted_iota(jnp.int32, (8, 128), 1)
    ar_send(CROSS, 0, jnp.where(lanes < 64, cross[:8], cross[8:]))

    def forward(s, carry):
        alive = jnp.where(s < live, 1.0, 0.0)
        h, l = split(column_rows(s) * alive)
        both = dot(jnp.concatenate([h, l], axis=0), high[s], 1, 1, None)
        products[s] = both[:K] + both[K:] + dot(h, low[s], 1, 1, None)
        return carry

    lax.fori_loop(0, SLOTS // 2, forward, 0, unroll=4)
    ar_next(CROSS, 0)
    lax.fori_loop(SLOTS // 2, SLOTS, forward, 0, unroll=4)

    def fill_core(half):
        def fill(yy, carry):
            pf[half, yy] = pick(yy * NC + half, rows_ref)
            return carry

        lax.fori_loop(0, NY, fill, 0)

    fill_core(1 - core)
    send_one("sc", pf.at[1 - core], rfc, other_core)
    ar_next(EARLY, 2)
    fill_core(core)
    scatter_z(0)
    arrived("sc", rfc)

    def sum_c(yy, carry):
        pf[core, yy] = pf[core, yy] + rfc[yy]
        return carry

    lax.fori_loop(0, NY, sum_c, 0)
    for index, device in y_peers:
        send("sy", pf.at[core, index], rfy.at[y], device)
    drains.append(("sy", pf.at[0, 0 : NY - 1]))
    ar_next(CROSS, 1)
    for h in range(1, len(SCATTER_GROUPS)):
        scatter_z(h)
    drains.append(("sz", rbz.at[0 : NZ - 1]))

    total_rows = BS * NZ * NX * NY * NC
    packed = ar_sum(EARLY, 3) / total_rows
    gram = jnp.concatenate([packed[:, 32 * i : 32 * i + 32] for i in range(4)], axis=0)
    squares = jnp.sum(gram[:K, :K] * identity(K), axis=1, keepdims=True)
    inverse = inverse_factor(gram[:K, :K], K)
    basis = dot(inverse, states)
    project = dot(gram[K:, :K], inverse, 1, 1)
    rest = directions - dot(project, basis)
    gram_rest = gram[K:, K:] - dot(project, project, 1, 1)
    loads[6].wait()
    rotation = rotation_ref[...]
    kept = dot(rotation[:, :K], basis)

    ar_next(CROSS, 2)
    arrived("sy", rfy.at[0 : NY - 1])
    applied = pf[core, y]
    for d in range(1, NY):
        applied = applied + rfy[lax.rem(y + d, NY)]
    arrived("sz", rbz.at[0 : NZ - 1])
    applied = applied + pb[x, 0]
    for place in range(1, NZ):
        applied = applied + rbz[place]
    crossed = ar_sum(CROSS, 3)
    quotient = jnp.concatenate([crossed[:, 0:1], crossed[:, 64:65]], axis=0) / (squares * total_rows)
    residual = applied - quotient * states

    left_side = jnp.concatenate([residual, rest], axis=0)
    right_side = jnp.concatenate([basis, residual, rest], axis=0)
    local = dot(left_side, right_side, 1, 1)
    wide = jnp.concatenate([local[:K], local[K:, K : 2 * K]], axis=1)
    ar_send(LATE, 0, jnp.concatenate([wide[:8], wide[8:]], axis=1))
    quotient_ref[...] = jnp.sum(identity(K) * quotient, axis=0, keepdims=True)
    ar_next(LATE, 0)

    def drain():
        for name, like in drains:
            pltpu.make_async_copy(like, like, send_sem.at[stage_of(name)]).wait()
        drains.clear()

    drain()
    ar_next(LATE, 1)
    ar_next(LATE, 2)
    packed = ar_sum(LATE, 3) / total_rows
    wide = jnp.concatenate([packed[:, :64], packed[:, 64:]], axis=0)
    lower = wide[:, :K]
    gram_residual = wide[:, K : 2 * K] - dot(lower, lower, 1, 1)
    top = jnp.concatenate([gram_residual, wide[:, 2 * K : 3 * K]], axis=1)
    bottom = jnp.concatenate([wide[:, 3 * K :], gram_rest], axis=1)
    inverse = inverse_factor(jnp.concatenate([top, bottom], axis=0), 2 * K)
    mixing = dot(rotation[:, K:], inverse)
    fresh = dot(mixing, jnp.concatenate([residual - dot(lower, basis), rest], axis=0))
    new_direction_ref[0] = fresh
    new_states_ref[0] = kept + new_direction_ref[0]

    drain()


def finish(states_hbm, direction_hbm, quotient_hbm, new_states_ref, new_direction_ref, quotient_ref, sem):
    copies = [
        pltpu.make_async_copy(states_hbm, new_states_ref, sem.at[0]),
        pltpu.make_async_copy(direction_hbm, new_direction_ref, sem.at[1]),
        pltpu.make_async_copy(quotient_hbm, quotient_ref, sem.at[2]),
    ]
    for copy in copies:
        copy.start()
    for copy in copies:
        copy.wait()


def body(states, direction, blocks, counts, block_rows, block_cols, rotation):
    vmem = pl.BlockSpec(memory_space=pltpu.VMEM)
    hbm = pl.BlockSpec(memory_space=pltpu.HBM)
    outs = (
        jax.ShapeDtypeStruct((1, K, BS), F32),
        jax.ShapeDtypeStruct((1, K, BS), F32),
        jax.ShapeDtypeStruct((1, K), F32),
    )
    results = pl.pallas_call(
        kernel,
        out_shape=outs,
        in_specs=[hbm] * 7,
        out_specs=(vmem, vmem, vmem),
        scratch_shapes=[
            pltpu.VMEM((SLOTS, BS, BS), F32),
            pltpu.VMEM((SLOTS, BS, BS), BF16),
            pltpu.VMEM((SLOTS, BS, BS), BF16),
            pltpu.VMEM((NX, NZ, K, BS), F32),
            pltpu.VMEM((NC, NY, K, BS), F32),
            pltpu.VMEM((SLOTS, K, BS), F32),
            pltpu.VMEM((NX, NZ, K, BS), F32),
            pltpu.VMEM((NC, NY, K, BS), F32),
            pltpu.VMEM((NX - 1, NZ, K, BS), F32),
            pltpu.VMEM((NZ, K, BS), F32),
            pltpu.VMEM((NY, K, BS), F32),
            pltpu.VMEM((NY, K, BS), F32),
            pltpu.VMEM((K, BS), F32),
            pltpu.VMEM((3, NC, 8, 128), F32),
            pltpu.VMEM((3, NX, 8, 128), F32),
            pltpu.VMEM((3, NY, 8, 128), F32),
            pltpu.VMEM((3, NZ, 8, 128), F32),
            pltpu.SMEM((1, 1), jnp.int32),
            pltpu.SMEM((1, 1, SLOTS), jnp.int32),
            pltpu.SMEM((1, 1, SLOTS), jnp.int32),
            pltpu.VMEM((K, NSUB), F32),
            pltpu.SemaphoreType.DMA((7,)),
            pltpu.SemaphoreType.DMA((SLOTS,)),
            pltpu.SemaphoreType.DMA((STAGES,)),
            pltpu.SemaphoreType.DMA((STAGES,)),
        ],
        compiler_params=pltpu.CompilerParams(
            collective_id=0, has_side_effects=True, vmem_limit_bytes=60 * 1024 * 1024
        ),
    )(states, direction, blocks, counts, block_rows, block_cols, rotation.T)
    new_states, new_direction, quotient = pl.pallas_call(
        finish,
        out_shape=outs,
        in_specs=[hbm] * 3,
        out_specs=(hbm,) * 3,
        scratch_shapes=[pltpu.SemaphoreType.DMA((3,))],
        compiler_params=pltpu.CompilerParams(vmem_limit_bytes=60 * 1024 * 1024),
    )(*results)
    return new_states, new_direction, quotient.reshape(K)


def solution(mesh):
    return jax.shard_map(
        body,
        mesh=mesh,
        in_specs=(
            P(("row", "col"), None, None),
            P(("row", "col"), None, None),
            P("row", "col", None, None, None),
            P("row", "col"),
            P("row", "col", None),
            P("row", "col", None),
            P(),
        ),
        out_specs=(P(("row", "col"), None, None), P(("row", "col"), None, None), P()),
        check_vma=False,
    )
```
